32 devices in a mesh: tiles: 8 (over z, y), rep: 4 (over x, core).
Axes of the slice: x: 2, y: 2, z: 4, core: 2. Of those that a mesh axis runs over, the one named last changes fastest.
Arguments:
- dissim: float32 [128, 128, 128], P(('tiles', 'rep')), may hold values from 0.5 to 4
- tile_map: int32 [128, 2], P(('tiles', 'rep')), may hold values from -1 to 7, as said below
- owned_blocks: int32 [8], P('tiles'), may hold values from 0 to 7, each once
- start_coords: float32 [8, 3, 128], P('tiles'), may hold values from -6 to 6
Outputs:
- coords: float32 [8, 3, 128], P('tiles')
- stress: float32 [], replicated
The draws below stay inside these ranges and needn't reach their ends.
Inputs may be any that keep to these rules, and one draw needn't show every extreme that they name: `tile_map`: every pair (r, c) with 0 <= r <= c < 8 stands in exactly one row; every other row is (-1, -1); the 4 rows of one device are filled by between 0 and 4 tiles, and one device is full.
All inputs are finite; a program needn't handle non-finite values.
Results may differ from the reference program's by a relative error of at most 0.0003.
Values sent between devices are 32-bit elements; how exact they have to be, the bound alone decides.
No kernel may reach another device: no remote copies, remote signals or barrier semaphores. Data moves between devices by JAX's collectives and lax.ppermute only.
A program may use at most 64 MiB of HBM per device.

```python
import jax
import jax.numpy as jnp
import numpy as np
from jax import lax

BLK = 128
ITERS = 3
NB = 8
SLOTS = 4
DEVICES = 32


def draw_tile_map(key, part):
    upper_rows, upper_cols = np.triu_indices(NB)
    pairs = jnp.asarray(np.stack([upper_rows, upper_cols], 1).astype(np.int32))
    triangle = int(upper_rows.shape[0])
    key_shift, key_rank, key_full, key_perm = jax.random.split(jax.random.fold_in(key, 7), 4)
    shifts = jax.random.randint(key_shift, (DEVICES,), 0, SLOTS // 2 + 1)
    ranking = jax.random.permutation(key_rank, DEVICES).astype(jnp.int32)
    full_device = jax.random.randint(key_full, (), 0, DEVICES)
    positions = jnp.arange(SLOTS, dtype=jnp.int32)
    devices = jnp.arange(DEVICES, dtype=jnp.int32)
    levels = positions[None, :] - shifts[:, None]
    scores = levels * DEVICES + ranking[:, None]
    scores = jnp.where(devices[:, None] == full_device, positions[None, :] - 4 * SLOTS * DEVICES, scores)
    ordering = jnp.argsort(scores.reshape(-1), stable=True)
    chosen = ordering[:triangle]
    shuffled = jax.random.permutation(key_perm, triangle)
    result = jnp.full((DEVICES * SLOTS, 2), -1, jnp.int32)
    return result.at[chosen].set(pairs[shuffled])


def block_scale(rng, shape, cuts, low, largest):
    def one(position, parts):
        draws = jax.random.uniform(jax.random.fold_in(jax.random.fold_in(rng, 6), position), (parts,), jnp.float32, low / len(cuts), largest / len(cuts))
        return jnp.repeat(jnp.exp(draws), shape[position] // parts).reshape((-1,) + (1,) * (len(shape) - position - 1))

    level = one(*cuts[0])
    for cut in cuts[1:]:
        level = level * one(*cut)
    return level


def centred(key, extent, width, bound, cuts=(), kind=jnp.bfloat16):
    array = jax.random.normal(key, extent, jnp.float32) * width
    if len(cuts) > 0:
        array = block_scale(key, extent, cuts, -0.22, 0.18) * array
    return jnp.clip(array, min=-bound, max=bound).astype(kind)


def setup_inputs(seed: int = 0) -> dict:
    arg_keys = jax.random.split(jax.random.key(seed), 5)
    dissim = jnp.clip(0.5 + 3.5 * jax.random.uniform(arg_keys[0], (DEVICES * SLOTS, BLK, BLK), jnp.float32) ** block_scale(arg_keys[0], (DEVICES * SLOTS, BLK, BLK), ((0, 32),), -0.2, 0.2), 0.5, 4.0)
    tile_map = draw_tile_map(jax.random.fold_in(arg_keys[4], 71), 0)
    owned_blocks = jax.random.permutation(arg_keys[2], NB).astype(jnp.int32)
    start_coords = centred(arg_keys[3], (NB, 3, BLK), 1.0, 6.0, ((0, 8),), jnp.float32)
    return dict(dissim=dissim, tile_map=tile_map, owned_blocks=owned_blocks, start_coords=start_coords)


distance_floor = 0.25

def tile_terms(coords_all, dissim, tile_map, slot_of):
    row_ids = tile_map[:, 0]
    col_ids = tile_map[:, 1]
    occupied = row_ids >= 0
    row_slot = slot_of[jnp.maximum(row_ids, 0)]
    col_slot = slot_of[jnp.maximum(col_ids, 0)]
    row_points = coords_all[row_slot]
    col_points = coords_all[col_slot]
    tile_width = dissim.shape[1]
    offsets = jnp.arange(tile_width, dtype=jnp.int32)
    above_diag = offsets[:, None] < offsets[None, :]
    kept_mask = occupied[:, None, None] & ((row_ids != col_ids)[:, None, None] | above_diag[None])
    squared = jnp.zeros(dissim.shape, jnp.float32)
    for component in range(3):
        spread = row_points[:, component, :, None] - col_points[:, component, None, :]
        squared = squared + spread * spread
    distance = jnp.sqrt(jnp.maximum(squared, distance_floor))
    ratios = jnp.where(kept_mask, dissim / distance, jnp.float32(0.0))
    misfit = jnp.where(kept_mask, (dissim - distance) ** 2, jnp.float32(0.0))
    stress = jnp.sum(misfit)
    row_total = lax.optimization_barrier(jnp.sum(ratios, axis=2))
    col_total = lax.optimization_barrier(jnp.sum(ratios, axis=1))
    row_terms = row_points * row_total[:, None, :] - jnp.einsum('sij,scj->sci', ratios, col_points, precision=lax.Precision.HIGHEST)
    col_terms = col_points * col_total[:, None, :] - jnp.einsum('sij,sci->scj', ratios, row_points, precision=lax.Precision.HIGHEST)
    block_count = coords_all.shape[0]
    totals = jnp.zeros((block_count, 3, tile_width), jnp.float32)
    totals = totals.at[row_slot].add(row_terms).at[col_slot].add(col_terms)
    return (totals, stress)

def reference(dissim, tile_map, owned_blocks, start_coords):
    block_count = owned_blocks.shape[0]
    slot_of = jnp.zeros((block_count,), jnp.int32).at[owned_blocks].set(jnp.arange(block_count, dtype=jnp.int32))
    tile_width = dissim.shape[1]
    grouped = dissim.reshape(DEVICES, SLOTS, tile_width, tile_width)
    grouped_map = tile_map.reshape(DEVICES, SLOTS, 2)
    coords_all = start_coords
    stress = jnp.float32(0.0)
    for step in range(ITERS):

        def accumulate(carry, pieces):
            totals, misfit = carry
            more, extra = tile_terms(coords_all, pieces[0], pieces[1], slot_of)
            return ((totals + more, misfit + extra), None)
        start = (jnp.zeros(coords_all.shape, jnp.float32), jnp.float32(0.0))
        (totals, stress), unused = lax.scan(accumulate, start, (grouped, grouped_map))
        coords_all = totals / jnp.float32(block_count * tile_width)
    return (coords_all, stress)
```

```python
import functools

import jax
import jax.numpy as jnp
from jax import lax
from jax.experimental import pallas as pl
from jax.experimental.pallas import tpu as pltpu
from jax.sharding import PartitionSpec as P

ITERS = 3
AXES = ("tiles", "rep")
distance_floor = 0.25
HIGHEST = lax.Precision.HIGHEST
DIRECT_BYTES = 1 << 20


def iteration(first, last, scaling, map_ref, dissim_ref, parts_ref, out_ref, coords, totals, misfit):
    slots, width = dissim_ref.shape[0], dissim_ref.shape[1]
    block_count = coords.shape[0]
    if first:
        owner = parts_ref[:, 3, :, :].reshape(-1, width)[:, :1]
        numbers = lax.broadcasted_iota(jnp.int32, (owner.shape[0], block_count), 1)
        placed = (owner.astype(jnp.int32) == numbers).astype(jnp.float32)
        components = [
            lax.dot_general(
                placed,
                parts_ref[:, k, :, :].reshape(-1, width),
                (((0,), (0,)), ((), ())),
                precision=HIGHEST,
                preferred_element_type=jnp.float32,
            )
            for k in range(3)
        ]
    else:
        components = [
            sum(parts_ref[p, k] for p in range(parts_ref.shape[0])) / scaling for k in range(3)
        ]
    row_of = lax.broadcasted_iota(jnp.int32, (8, width), 0)
    for b in range(block_count):
        rows = jnp.where(row_of == 3, jnp.float32(1.0), jnp.float32(0.0))
        for k in range(3):
            rows = jnp.where(row_of == k, components[k][b : b + 1], rows)
        coords[b] = rows
    totals[...] = jnp.zeros_like(totals)
    if last:
        misfit[...] = jnp.zeros_like(misfit)
    above_diag = lax.broadcasted_iota(jnp.int32, (width, width), 0) < lax.broadcasted_iota(
        jnp.int32, (width, width), 1
    )
    for s in range(slots):
        row, col = map_ref[s, 0], map_ref[s, 1]

        @pl.when(row >= 0)
        def _():
            row_points, col_points = coords[row], coords[col]
            columns = row_points.T
            squared = jnp.zeros((width, width), jnp.float32)
            for k in range(3):
                spread = columns[:, k : k + 1] - col_points[k : k + 1, :]
                squared = squared + spread * spread
            squared = jnp.maximum(squared, distance_floor)
            inverse = lax.rsqrt(squared)
            kept = above_diag | (row != col)
            delta = dissim_ref[s]
            ratios = jnp.where(kept, delta * inverse, jnp.float32(0.0))
            if last:
                off = jnp.where(kept, delta - squared * inverse, jnp.float32(0.0))
                misfit[...] += jnp.sum((off * off).reshape(-1, 8, width), axis=0)
            to_rows = lax.dot_general(
                col_points, ratios, (((1,), (1,)), ((), ())), precision=HIGHEST, preferred_element_type=jnp.float32
            )
            to_cols = lax.dot_general(
                row_points, ratios, (((1,), (0,)), ((), ())), precision=HIGHEST, preferred_element_type=jnp.float32
            )
            totals[row] += row_points * to_rows[3:4] - to_rows
            totals[col] += col_points * to_cols[3:4] - to_cols

    for k in range(3):
        out_ref[k] = totals[:, k, :]
    if last:
        out_ref[3, :8] = misfit[...]
        if block_count > 8:
            out_ref[3, 8:] = jnp.zeros((block_count - 8, width), jnp.float32)


def contributions(first, last, scaling, block_count, tile_map, dissim, parts):
    width = dissim.shape[1]
    return pl.pallas_call(
        functools.partial(iteration, first, last, scaling),
        out_shape=jax.ShapeDtypeStruct((4 if last else 3, block_count, width), jnp.float32),
        in_specs=[
            pl.BlockSpec(memory_space=pltpu.SMEM),
            pl.BlockSpec(memory_space=pltpu.VMEM),
            pl.BlockSpec(memory_space=pltpu.VMEM),
        ],
        out_specs=pl.BlockSpec(memory_space=pltpu.VMEM),
        scratch_shapes=[
            pltpu.VMEM((block_count, 8, width), jnp.float32),
            pltpu.VMEM((block_count, 8, width), jnp.float32),
            pltpu.VMEM((8, width), jnp.float32),
        ],
        compiler_params=pltpu.CompilerParams(vmem_limit_bytes=32 << 20),
        name="iteration",
    )(tile_map, dissim, parts)


def gathered(message, axis, count, groups=None):
    copies = jnp.broadcast_to(message[None], (count, *message.shape))
    return lax.all_to_all(copies, axis, 0, 0, axis_index_groups=groups)


def exchanged(message, tiles, rep):
    if rep % 2 or tiles * rep // 2 * message.size * 4 > DIRECT_BYTES:
        return lax.psum(message, AXES)[None]
    message = message + lax.ppermute(message, AXES, [(i, i ^ 1) for i in range(tiles * rep)])
    count = tiles * rep // 2
    groups = [[2 * i + core for i in range(count)] for core in range(2)]
    return gathered(message, AXES, count, groups)


def local(tiles, rep, dissim, tile_map, owned_blocks, start_coords):
    owned_count, _, width = start_coords.shape
    block_count = owned_count * tiles
    scaling = float(block_count * width)
    named = jnp.broadcast_to(owned_blocks.astype(jnp.float32)[None, :, None], (1, owned_count, width))
    message = jnp.concatenate([start_coords.swapaxes(0, 1), named])
    parts = gathered(message, "tiles", tiles)
    for step in range(ITERS):
        last = step == ITERS - 1
        totals = contributions(step == 0, last, scaling, block_count, tile_map, dissim, parts)
        parts = exchanged(totals, tiles, rep)
    stress = jnp.sum(parts[:, 3])
    coords = jnp.sum(parts[:, :3], axis=0) / scaling
    mine = (owned_blocks[:, None] == jnp.arange(block_count)[None]).astype(jnp.float32)
    owned = jnp.sum(mine[:, None, :, None] * coords[None], axis=2)
    return owned, stress


def solution(mesh):
    return jax.shard_map(
        functools.partial(local, mesh.shape["tiles"], mesh.shape["rep"]),
        mesh=mesh,
        in_specs=(
            P(AXES, None, None),
            P(AXES, None),
            P("tiles"),
            P("tiles", None, None),
        ),
        out_specs=(P("tiles", None, None), P()),
        check_vma=False,
    )
```

```python
import functools

import jax
import jax.numpy as jnp
from jax import lax
from jax.experimental import pallas as pl
from jax.experimental.pallas import tpu as pltpu
from jax.sharding import PartitionSpec as P

ITERS = 3
AXES = ("tiles", "rep")
distance_floor = 0.25
HIGHEST = lax.Precision.HIGHEST
DIRECT_BYTES = 1 << 20
GROUP_BYTES = 2 << 20


def iteration(first, last, scaling, map_ref, dissim_ref, *refs):
    *parts, out_ref, coords, totals, misfit = refs
    parts_ref = parts[0]
    slots, width = dissim_ref.shape[0], dissim_ref.shape[1]
    block_count = coords.shape[0]
    if first:
        owner = parts_ref[:, 3, :, :].reshape(-1, width)[:, :1]
        numbers = lax.broadcasted_iota(jnp.int32, (owner.shape[0], block_count), 1)
        placed = (owner.astype(jnp.int32) == numbers).astype(jnp.float32)
        components = [
            lax.dot_general(
                placed,
                parts_ref[:, k, :, :].reshape(-1, width),
                (((0,), (0,)), ((), ())),
                precision=HIGHEST,
                preferred_element_type=jnp.float32,
            )
            for k in range(3)
        ]
    else:
        components = [
            sum(part[p, k] for part in parts for p in range(part.shape[0])) / scaling for k in range(3)
        ]
    row_of = lax.broadcasted_iota(jnp.int32, (8, width), 0)
    for b in range(block_count):
        rows = jnp.where(row_of == 3, jnp.float32(1.0), jnp.float32(0.0))
        for k in range(3):
            rows = jnp.where(row_of == k, components[k][b : b + 1], rows)
        coords[b] = rows
    totals[...] = jnp.zeros_like(totals)
    if last:
        misfit[...] = jnp.zeros_like(misfit)
    above_diag = lax.broadcasted_iota(jnp.int32, (width, width), 0) < lax.broadcasted_iota(
        jnp.int32, (width, width), 1
    )
    for s in range(slots):
        row, col = map_ref[s, 0], map_ref[s, 1]

        @pl.when(row >= 0)
        def _():
            row_points, col_points = coords[row], coords[col]
            columns = row_points.T
            squared = jnp.zeros((width, width), jnp.float32)
            for k in range(3):
                spread = columns[:, k : k + 1] - col_points[k : k + 1, :]
                squared = squared + spread * spread
            squared = jnp.maximum(squared, distance_floor)
            inverse = lax.rsqrt(squared)
            kept = above_diag | (row != col)
            delta = dissim_ref[s]
            ratios = jnp.where(kept, delta * inverse, jnp.float32(0.0))
            if last:
                off = jnp.where(kept, delta - squared * inverse, jnp.float32(0.0))
                misfit[...] += jnp.sum((off * off).reshape(-1, 8, width), axis=0)
            to_rows = lax.dot_general(
                col_points, ratios, (((1,), (1,)), ((), ())), precision=HIGHEST, preferred_element_type=jnp.float32
            )
            to_cols = lax.dot_general(
                row_points, ratios, (((1,), (0,)), ((), ())), precision=HIGHEST, preferred_element_type=jnp.float32
            )
            totals[row] += row_points * to_rows[3:4] - to_rows
            totals[col] += col_points * to_cols[3:4] - to_cols

    for k in range(3):
        out_ref[k] = totals[:, k, :]
    if last:
        out_ref[3, :8] = misfit[...]
        if block_count > 8:
            out_ref[3, 8:] = jnp.zeros((block_count - 8, width), jnp.float32)


def contributions(first, last, scaling, block_count, tile_map, dissim, parts):
    width = dissim.shape[1]
    return pl.pallas_call(
        functools.partial(iteration, first, last, scaling),
        out_shape=jax.ShapeDtypeStruct((4 if last else 3, block_count, width), jnp.float32),
        in_specs=[
            pl.BlockSpec(memory_space=pltpu.SMEM),
            *[pl.BlockSpec(memory_space=pltpu.VMEM)] * (1 + len(parts)),
        ],
        out_specs=pl.BlockSpec(memory_space=pltpu.VMEM),
        scratch_shapes=[
            pltpu.VMEM((block_count, 8, width), jnp.float32),
            pltpu.VMEM((block_count, 8, width), jnp.float32),
            pltpu.VMEM((8, width), jnp.float32),
        ],
        compiler_params=pltpu.CompilerParams(vmem_limit_bytes=32 << 20),
        name="iteration",
    )(tile_map, dissim, *parts)


def gathered(message, axis, count, groups=None):
    copies = jnp.broadcast_to(message[None], (count, *message.shape))
    return lax.all_to_all(copies, axis, 0, 0, axis_index_groups=groups)


def moved(array, devices, distance):
    return lax.ppermute(array, AXES, [(i, i ^ distance) for i in range(devices)])


def exchanged(message, devices, group):
    if group > 1:
        return [message[None]] + [moved(message[None], devices, k) for k in range(group, devices, group)]
    if devices % 2 or devices // 2 * message.size * 4 > DIRECT_BYTES:
        return [lax.psum(message, AXES)[None]]
    message = message + moved(message, devices, 1)
    count = devices // 2
    groups = [[2 * i + core for i in range(count)] for core in range(2)]
    return [gathered(message, AXES, count, groups)]


def group_of(tiles, rep, tile_bytes):
    devices = tiles * rep
    if devices & (devices - 1):
        return 1
    group = devices
    while group > 1 and group * tile_bytes > GROUP_BYTES:
        group //= 2
    return group if 1 < rep <= group and devices // group <= 8 else 1


def local(tiles, rep, dissim, tile_map, owned_blocks, start_coords):
    owned_count, _, width = start_coords.shape
    slots = dissim.shape[0]
    devices = tiles * rep
    block_count = owned_count * tiles
    scaling = float(block_count * width)
    named = jnp.broadcast_to(owned_blocks.astype(jnp.float32)[None, :, None], (1, owned_count, width))
    message = jnp.concatenate([start_coords.swapaxes(0, 1), named])
    group = group_of(tiles, rep, dissim.size * 4)
    if group > 1:
        numbers = tile_map.astype(jnp.float32).reshape(1, 2 * slots)
        packed = jnp.concatenate([dissim.reshape(-1, width), jnp.pad(numbers, ((0, 7), (0, width - 2 * slots)))])
        packs = [packed] + [moved(packed, devices, k) for k in range(2, group, 2)]
        parts = jnp.stack([message] + [moved(message, devices, k) for k in range(group, devices, group)])
        parts = [jnp.concatenate([parts] + [moved(parts, devices, k) for k in range(rep, group, rep)])]
        packs += [moved(pack, devices, 1) for pack in packs]
        dissim = jnp.concatenate([pack[:-8].reshape(slots, width, width) for pack in packs])
        tile_map = jnp.concatenate([pack[-8, : 2 * slots].astype(jnp.int32).reshape(slots, 2) for pack in packs])
    else:
        parts = [gathered(message, "tiles", tiles)]
    for step in range(ITERS):
        last = step == ITERS - 1
        totals = contributions(step == 0, last, scaling, block_count, tile_map, dissim, parts)
        parts = exchanged(totals, devices, group)
    summed = sum(jnp.sum(part, axis=0) for part in parts)
    stress = jnp.sum(summed[3])
    mine = (owned_blocks[:, None] == jnp.arange(block_count)[None]).astype(jnp.float32)
    owned = jnp.sum(mine[:, None, :, None] * (summed[:3] / scaling)[None], axis=2)
    return owned, stress


def solution(mesh):
    return jax.shard_map(
        functools.partial(local, mesh.shape["tiles"], mesh.shape["rep"]),
        mesh=mesh,
        in_specs=(
            P(AXES, None, None),
            P(AXES, None),
            P("tiles"),
            P("tiles", None, None),
        ),
        out_specs=(P("tiles", None, None), P()),
        check_vma=False,
    )
```

```python
import functools

import jax
import jax.numpy as jnp
from jax import lax
from jax.experimental import pallas as pl
from jax.experimental.pallas import tpu as pltpu
from jax.sharding import PartitionSpec as P

ITERS = 3
AXES = ("tiles", "rep")
distance_floor = 0.25
DIRECT_BYTES = 1 << 20
SHARED_BYTES = 2 << 20
BATCH = 4


def pieces(array, count):
    found = []
    for _ in range(count):
        piece = array.astype(jnp.bfloat16)
        found.append(piece)
        array = array - piece.astype(jnp.float32)
    return found


def products(points, ratios, axis):
    left = jnp.concatenate([piece.astype(jnp.float32) for piece in pieces(points, 3)]).astype(jnp.bfloat16)
    right = jnp.concatenate(ratios, axis=axis)
    split = lax.dot_general(
        jnp.concatenate([left] * len(ratios), axis=1),
        right,
        (((1,), (axis,)), ((), ())),
        preferred_element_type=jnp.float32,
    )
    return split[:8] + split[8:16] + split[16:]


def tile_terms(row_points, col_points, delta, kept, last):
    width = delta.shape[0]
    columns = row_points.T
    squared = jnp.zeros((width, width), jnp.float32)
    for k in range(3):
        spread = columns[:, k : k + 1] - col_points[k : k + 1, :]
        squared = squared + spread * spread
    squared = jnp.maximum(squared, distance_floor)
    inverse = lax.rsqrt(squared)
    ratios = jnp.where(kept, delta * inverse, jnp.float32(0.0))
    off = None
    if last:
        off = jnp.where(kept, delta - squared * inverse, jnp.float32(0.0))
        off = jnp.sum((off * off).reshape(-1, 8, width), axis=0)
    ratios = pieces(ratios, 2)
    to_rows = products(col_points, ratios, 1)
    to_cols = products(row_points, ratios, 0)
    return row_points * to_rows[3:4] - to_rows, col_points * to_cols[3:4] - to_cols, off


def iteration(first, last, scaling, map_ref, dissim_ref, *refs):
    *parts, out_ref, coords, totals, misfit, filled = refs
    slots, width = dissim_ref.shape[0], dissim_ref.shape[1]
    block_count = coords.shape[0]

    def note(s, count):
        filled[count] = s
        return count + (map_ref[0, s] >= 0).astype(jnp.int32)

    count = lax.fori_loop(0, slots, note, jnp.int32(0), unroll=min(slots, 16))
    for j in range(BATCH):
        filled[count + j] = 0
    if first:
        parts_ref = parts[0]
        owner = parts_ref[:, 3, :, :].reshape(-1, width)[:, :1]
        numbers = lax.broadcasted_iota(jnp.int32, (owner.shape[0], block_count), 1)
        placed = (owner.astype(jnp.int32) == numbers).astype(jnp.float32)
        components = [
            lax.dot_general(
                placed,
                parts_ref[:, k, :, :].reshape(-1, width),
                (((0,), (0,)), ((), ())),
                precision=lax.Precision.HIGHEST,
                preferred_element_type=jnp.float32,
            )
            for k in range(3)
        ]
    else:
        components = [
            sum(part[p, k] for part in parts for p in range(part.shape[0])) / scaling for k in range(3)
        ]
    row_of = lax.broadcasted_iota(jnp.int32, (8, width), 0)
    for b in range(block_count):
        rows = jnp.where(row_of == 3, jnp.float32(1.0), jnp.float32(0.0))
        for k in range(3):
            rows = jnp.where(row_of == k, components[k][b : b + 1], rows)
        coords[b] = rows
    totals[...] = jnp.zeros_like(totals)
    if last:
        misfit[...] = jnp.zeros_like(misfit)
    above_diag = lax.broadcasted_iota(jnp.int32, (width, width), 0) < lax.broadcasted_iota(
        jnp.int32, (width, width), 1
    )

    def batch(i, carry):
        found = []
        for j in range(BATCH):
            place = i * BATCH + j
            s = filled[place]
            row, col = jnp.maximum(map_ref[0, s], 0), jnp.maximum(map_ref[1, s], 0)
            kept = (above_diag | (row != col)) & (place < count)
            found.append((row, col, *tile_terms(coords[row], coords[col], dissim_ref[s], kept, last)))
        for row, col, to_row, to_col, off in found:
            totals[row] += to_row
            totals[col] += to_col
            if last:
                misfit[...] += off
        return carry

    lax.fori_loop(0, (count + BATCH - 1) // BATCH, batch, 0)
    for k in range(3):
        out_ref[k] = totals[:, k, :]
    if last:
        out_ref[3, :8] = misfit[...]
        if block_count > 8:
            out_ref[3, 8:] = jnp.zeros((block_count - 8, width), jnp.float32)


def contributions(first, last, scaling, block_count, tile_map, dissim, parts):
    slots, width = dissim.shape[:2]
    return pl.pallas_call(
        functools.partial(iteration, first, last, scaling),
        out_shape=jax.ShapeDtypeStruct((4 if last else 3, block_count, width), jnp.float32),
        in_specs=[
            pl.BlockSpec(memory_space=pltpu.SMEM),
            *[pl.BlockSpec(memory_space=pltpu.VMEM)] * (1 + len(parts)),
        ],
        out_specs=pl.BlockSpec(memory_space=pltpu.VMEM),
        scratch_shapes=[
            pltpu.VMEM((block_count, 8, width), jnp.float32),
            pltpu.VMEM((block_count, 8, width), jnp.float32),
            pltpu.VMEM((8, width), jnp.float32),
            pltpu.SMEM((slots + BATCH,), jnp.int32),
        ],
        compiler_params=pltpu.CompilerParams(vmem_limit_bytes=32 << 20),
        name="iteration",
    )(tile_map, dissim, *parts)


def gathered(message, axis, count, groups=None):
    copies = jnp.broadcast_to(message[None], (count, *message.shape))
    return lax.all_to_all(copies, axis, 0, 0, axis_index_groups=groups)


def moved(array, devices, distance):
    return lax.ppermute(array, AXES, [(i, i ^ distance) for i in range(devices)])


def moved(array, devices, distance):
    return lax.ppermute(array, AXES, [(i, i ^ distance) for i in range(devices)])


def exchanged(message, tiles, rep, shared):
    devices = tiles * rep
    if shared:
        return [gathered(message, "tiles", tiles)]
    if devices % 2 or devices // 2 * message.size * 4 > DIRECT_BYTES:
        return [lax.psum(message, AXES)[None]]
    message = message + moved(message, devices, 1)
    count = devices // 2
    groups = [[2 * i + core for i in range(count)] for core in range(2)]
    return [gathered(message, AXES, count, groups)]


def doubled(array, devices, rep, axis):
    bit = rep // 2
    while bit:
        array = jnp.concatenate([array, moved(array, devices, bit)], axis=axis)
        bit //= 2
    return array


def start_points(message, tiles, rep):
    devices = tiles * rep
    if tiles & (tiles - 1) or rep % 2 or not 2 <= tiles <= 8:
        return gathered(message, "tiles", tiles)
    even = lax.axis_index("rep") % 2 == 0
    found = []
    for k in range(0, tiles, 2):
        pairs = [(i, i ^ rep * (k + i % 2)) for i in range(devices)]
        found.append(lax.ppermute(message, AXES, [(i, j) for i, j in pairs if i != j]))
    found[0] = jnp.where(even, message, found[0])
    half = jnp.stack(found)
    return jnp.concatenate([half, moved(half, devices, 1)])


def local(tiles, rep, dissim, tile_map, owned_blocks, start_coords):
    owned_count, _, width = start_coords.shape
    devices = tiles * rep
    block_count = owned_count * tiles
    scaling = float(block_count * width)
    named = jnp.broadcast_to(owned_blocks.astype(jnp.float32)[None, :, None], (1, owned_count, width))
    message = jnp.concatenate([start_coords.swapaxes(0, 1), named])
    tile_map = tile_map.T
    shared = 1 < rep and not rep & (rep - 1) and rep * dissim.size * 4 <= SHARED_BYTES
    if shared:
        dissim = doubled(dissim, devices, rep, 0)
        tile_map = doubled(tile_map, devices, rep, 1)
    parts = [start_points(message, tiles, rep)]
    for step in range(ITERS):
        last = step == ITERS - 1
        totals = contributions(step == 0, last, scaling, block_count, tile_map, dissim, parts)
        parts = exchanged(totals, tiles, rep, shared)
    summed = sum(jnp.sum(part, axis=0) for part in parts)
    stress = jnp.sum(summed[3])
    mine = (owned_blocks[:, None] == jnp.arange(block_count)[None]).astype(jnp.float32)
    owned = jnp.sum(mine[:, None, :, None] * (summed[:3] / scaling)[None], axis=2)
    return owned, stress


def solution(mesh):
    return jax.shard_map(
        functools.partial(local, mesh.shape["tiles"], mesh.shape["rep"]),
        mesh=mesh,
        in_specs=(
            P(AXES, None, None),
            P(AXES, None),
            P("tiles"),
            P("tiles", None, None),
        ),
        out_specs=(P("tiles", None, None), P()),
        check_vma=False,
    )
```

```python
import functools

import jax
import jax.numpy as jnp
from jax import lax
from jax.experimental import pallas as pl
from jax.experimental.pallas import tpu as pltpu
from jax.sharding import PartitionSpec as P

ITERS = 3
AXES = ("tiles", "rep")
distance_floor = 0.25
DIRECT_BYTES = 1 << 20
SHARED_BYTES = 2 << 20
EXTRA = 8
PACKED = [
    (4 * core + device, 2 * half + slot)
    for core in range(2)
    for half, pair in ((0, (0, 1)), (1, (0, 2)), (0, (2, 3)), (1, (1, 3)))
    for device in pair
    for slot in range(2)
]
BATCH = 4


def pieces(array, count):
    found = []
    for _ in range(count):
        piece = array.astype(jnp.bfloat16)
        found.append(piece)
        array = array - piece.astype(jnp.float32)
    return found


def products(points, ratios, axis):
    left = jnp.concatenate([piece.astype(jnp.float32) for piece in pieces(points, 3)]).astype(jnp.bfloat16)
    right = jnp.concatenate(ratios, axis=axis)
    split = lax.dot_general(
        jnp.concatenate([left] * len(ratios), axis=1),
        right,
        (((1,), (axis,)), ((), ())),
        preferred_element_type=jnp.float32,
    )
    return split[:8] + split[8:16] + split[16:]


def tile_terms(row_points, col_points, delta, kept, last):
    width = delta.shape[0]
    columns = row_points.T
    squared = jnp.zeros((width, width), jnp.float32)
    for k in range(3):
        spread = columns[:, k : k + 1] - col_points[k : k + 1, :]
        squared = squared + spread * spread
    squared = jnp.maximum(squared, distance_floor)
    inverse = lax.rsqrt(squared)
    ratios = jnp.where(kept, delta * inverse, jnp.float32(0.0))
    off = None
    if last:
        off = jnp.where(kept, delta - squared * inverse, jnp.float32(0.0))
        off = jnp.sum((off * off).reshape(-1, 8, width), axis=0)
    ratios = pieces(ratios, 2)
    to_rows = products(col_points, ratios, 1)
    to_cols = products(row_points, ratios, 0)
    return row_points * to_rows[3:4] - to_rows, col_points * to_cols[3:4] - to_cols, off


def placed(messages, block_count):
    blocks = []
    for b in range(block_count):
        found = jnp.zeros_like(messages[0])
        for message in messages:
            found = found + jnp.where(message[3:4] == b, message, jnp.float32(0.0))
        blocks.append(found)
    return blocks


def iteration(packed, first, last, scaling, map_ref, dissim_ref, *refs):
    *parts, out_ref, coords, totals, misfit, row_list, col_list, place_list = refs
    block_count, width = coords.shape[0], coords.shape[2]

    def note(count, device, slot, place):
        row = map_ref[2 * device, slot]
        row_list[count] = row
        col_list[count] = map_ref[2 * device + 1, slot]
        place_list[count] = place
        return count + (row >= 0).astype(jnp.int32)

    count = jnp.int32(0)
    if packed:
        for n, (device, slot) in enumerate(PACKED):
            count = note(count, device, slot, n * width + n // 2 * EXTRA)
    else:
        count = lax.fori_loop(0, map_ref.shape[1], lambda s, count: note(count, 0, s, s * width), count)
    for j in range(BATCH):
        row_list[count + j] = 0
        col_list[count + j] = 0
        place_list[count + j] = 0
    row_of = lax.broadcasted_iota(jnp.int32, (8, width), 0)
    if first:
        blocks = placed([part[m] for part in parts for m in range(part.shape[0])], block_count)
    else:
        components = [
            sum(part[p, k] for part in parts for p in range(part.shape[0])) / scaling for k in range(3)
        ]
    for b in range(block_count):
        if first:
            rows = blocks[b]
        else:
            rows = components[2][b : b + 1]
            for k in (1, 0):
                rows = jnp.where(row_of == k, components[k][b : b + 1], rows)
        coords[b] = jnp.where(row_of < 3, rows, jnp.where(row_of == 3, jnp.float32(1.0), jnp.float32(0.0)))
    totals[...] = jnp.zeros_like(totals)
    if last:
        misfit[...] = jnp.zeros_like(misfit)
    above_diag = lax.broadcasted_iota(jnp.int32, (width, width), 0) < lax.broadcasted_iota(
        jnp.int32, (width, width), 1
    )

    def batch(i, carry):
        found = []
        for j in range(BATCH):
            n = i * BATCH + j
            row, col = row_list[n], col_list[n]
            kept = (above_diag | (row != col)) & (n < count)
            delta = dissim_ref[pl.ds(pl.multiple_of(place_list[n], 8), width)]
            found.append((row, col, *tile_terms(coords[row], coords[col], delta, kept, last)))
        for row, col, to_row, to_col, off in found:
            totals[row] += to_row
            totals[col] += to_col
            if last:
                misfit[...] += off
        return carry

    lax.fori_loop(0, (count + BATCH - 1) // BATCH, batch, 0)
    for k in range(3):
        out_ref[0, k] = totals[:, k, :]
    if last:
        out_ref[0, 3, :8] = misfit[...]
        if block_count > 8:
            out_ref[0, 3, 8:] = jnp.zeros((block_count - 8, width), jnp.float32)


def contributions(packed, first, last, scaling, block_count, tile_map, dissim, parts):
    slots, width = tile_map.size // 2, dissim.shape[1]
    return pl.pallas_call(
        functools.partial(iteration, packed, first, last, scaling),
        out_shape=jax.ShapeDtypeStruct((1, 4 if last else 3, block_count, width), jnp.float32),
        in_specs=[
            pl.BlockSpec(memory_space=pltpu.SMEM),
            *[pl.BlockSpec(memory_space=pltpu.VMEM)] * (1 + len(parts)),
        ],
        out_specs=pl.BlockSpec(memory_space=pltpu.VMEM),
        scratch_shapes=[
            pltpu.VMEM((block_count, 8, width), jnp.float32),
            pltpu.VMEM((block_count, 8, width), jnp.float32),
            pltpu.VMEM((8, width), jnp.float32),
            *[pltpu.SMEM((slots + BATCH,), jnp.int32)] * 3,
        ],
        compiler_params=pltpu.CompilerParams(vmem_limit_bytes=32 << 20),
        name="iteration",
    )(tile_map, dissim, *parts)


def pack(map_ref, owned_ref, dissim_ref, start_ref, a_ref, b_ref, sem):
    rows = a_ref.shape[0] - EXTRA
    copies = [
        pltpu.make_async_copy(dissim_ref.at[pl.ds(h * rows, rows)], ref.at[pl.ds(0, rows)], sem.at[h])
        for h, ref in enumerate((a_ref, b_ref))
    ]
    for copy in copies:
        copy.start()
    shape = (EXTRA, a_ref.shape[1])
    lane = lax.broadcasted_iota(jnp.int32, shape, 1)
    row_of = lax.broadcasted_iota(jnp.int32, shape, 0)
    numbers = jnp.zeros(shape, jnp.int32)
    slots = map_ref.shape[1]
    for s in range(slots):
        for k in range(2):
            numbers = jnp.where((lane == s) & (row_of == k), map_ref[k, s], numbers)
    a_ref[rows:] = numbers.astype(jnp.float32)
    message = jnp.zeros(shape, jnp.float32)
    for k in range(3):
        message = jnp.where(row_of == k, start_ref[k], message)
    b_ref[rows:] = jnp.where(row_of == 3, owned_ref[0].astype(jnp.float32), message)
    for copy in copies:
        copy.wait()


def packs(tile_map, owned_blocks, dissim, start_coords):
    rows, width = dissim.shape[0] // 2 + EXTRA, dissim.shape[1]
    return pl.pallas_call(
        pack,
        out_shape=[jax.ShapeDtypeStruct((rows, width), jnp.float32)] * 2,
        in_specs=[
            pl.BlockSpec(memory_space=pltpu.SMEM),
            pl.BlockSpec(memory_space=pltpu.SMEM),
            pl.BlockSpec(memory_space=pl.ANY),
            pl.BlockSpec(memory_space=pltpu.VMEM),
        ],
        out_specs=[pl.BlockSpec(memory_space=pltpu.VMEM)] * 2,
        scratch_shapes=[pltpu.SemaphoreType.DMA((2,))],
        compiler_params=pltpu.CompilerParams(vmem_limit_bytes=8 << 20),
        name="pack",
    )(tile_map, owned_blocks, dissim, start_coords)


def finish(scaling, owned_ref, *refs):
    *parts, coords_ref, stress_ref = refs
    summed = [sum(part[p, k] for part in parts for p in range(part.shape[0])) for k in range(4)]
    row_of = lax.broadcasted_iota(jnp.int32, summed[0].shape, 0)
    for o in range(coords_ref.shape[1]):
        for k in range(3):
            mine = jnp.where(row_of == owned_ref[o], summed[k], jnp.float32(0.0))
            coords_ref[k, o : o + 1] = jnp.sum(mine, axis=0, keepdims=True) / scaling
    stress_ref[0, 0] = jnp.sum(summed[3])


def results(scaling, owned_blocks, parts):
    owned_count, width = owned_blocks.shape[0], parts[0].shape[-1]
    coords, stress = pl.pallas_call(
        functools.partial(finish, scaling),
        out_shape=[
            jax.ShapeDtypeStruct((3, owned_count, width), jnp.float32),
            jax.ShapeDtypeStruct((1, 1), jnp.float32),
        ],
        in_specs=[
            pl.BlockSpec(memory_space=pltpu.SMEM),
            *[pl.BlockSpec(memory_space=pltpu.VMEM)] * len(parts),
        ],
        out_specs=[pl.BlockSpec(memory_space=pltpu.VMEM), pl.BlockSpec(memory_space=pltpu.SMEM)],
        compiler_params=pltpu.CompilerParams(vmem_limit_bytes=8 << 20),
        name="finish",
    )(owned_blocks, *parts)
    return coords.swapaxes(0, 1), stress.reshape(())


def gathered(message, axis, count, groups=None):
    copies = jnp.broadcast_to(message[None], (count, *message.shape))
    return lax.all_to_all(copies, axis, 0, 0, axis_index_groups=groups)


def moved(array, devices, distance):
    return lax.ppermute(array, AXES, [(i, i ^ distance) for i in range(devices)])


def moved(array, devices, distance):
    return lax.ppermute(array, AXES, [(i, i ^ distance) for i in range(devices)])


def moved(array, devices, distance):
    return lax.ppermute(array, AXES, [(i, i ^ distance) for i in range(devices)])


def exchanged(message, tiles, rep, group):
    devices = tiles * rep
    if group > 1:
        return [message] + [moved(message, devices, k) for k in range(group, devices, group)]
    if devices % 2 or devices // 2 * message.size * 4 > DIRECT_BYTES:
        return [lax.psum(message, AXES)]
    message = message[0] + moved(message[0], devices, 1)
    count = devices // 2
    groups = [[2 * i + core for i in range(count)] for core in range(2)]
    return [gathered(message, AXES, count, groups)]


def shared(tile_map, owned_blocks, dissim, start_coords, devices, rep):
    far, other = rep // 2, rep
    slots, width = dissim.shape[:2]
    a, b = packs(tile_map, owned_blocks, dissim.reshape(-1, width), start_coords.swapaxes(0, 1))
    a = jnp.stack([a, moved(a, devices, far)])
    b = jnp.stack([b, moved(b, devices, other)])
    parts = [b[:, -EXTRA:]]
    parts += [moved(parts[0], devices, k) for k in range(2 * rep, devices, 2 * rep)]
    halves = [a, b, moved(a, devices, other), moved(b, devices, far)]
    halves += [moved(half, devices, 1) for half in halves]
    maps = jnp.concatenate(halves[::2])[:, -EXTRA : 2 - EXTRA, :slots].astype(jnp.int32)
    return maps.reshape(-1, slots), jnp.concatenate(halves).reshape(-1, width), parts


def local(tiles, rep, dissim, tile_map, owned_blocks, start_coords):
    owned_count, _, width = start_coords.shape
    slots = dissim.shape[0]
    devices = tiles * rep
    block_count = owned_count * tiles
    scaling = float(block_count * width)
    tile_map = tile_map.T
    fits = 2 * rep * dissim.size * 4 <= SHARED_BYTES
    if fits and (slots, rep, owned_count) == (4, 4, 1) and tiles in (2, 4, 8):
        group = 2 * rep
        tile_map, dissim, parts = shared(tile_map, owned_blocks, dissim, start_coords, devices, rep)
    else:
        group = 1
        named = lax.all_gather(owned_blocks, "tiles", tiled=True)
        parts = lax.all_gather(start_coords, "tiles", tiled=True)
        put = (named[None] == jnp.arange(block_count)[:, None]).astype(jnp.float32)
        parts = [jnp.einsum("bk,kcp->cbp", put, parts, precision=lax.Precision.HIGHEST)[None]]
        dissim = dissim.reshape(-1, width)
    for step in range(ITERS):
        first, last = step == 0, step == ITERS - 1
        totals = contributions(
            group > 1, group > 1 and first, last, 1.0 if first else scaling, block_count, tile_map, dissim, parts
        )
        parts = exchanged(totals, tiles, rep, group)
    return results(scaling, owned_blocks, parts)


def solution(mesh):
    return jax.shard_map(
        functools.partial(local, mesh.shape["tiles"], mesh.shape["rep"]),
        mesh=mesh,
        in_specs=(
            P(AXES, None, None),
            P(AXES, None),
            P("tiles"),
            P("tiles", None, None),
        ),
        out_specs=(P("tiles", None, None), P()),
        check_vma=False,
    )
```

```python
import functools

import jax
import jax.numpy as jnp
from jax import lax
from jax.experimental import pallas as pl
from jax.experimental.pallas import tpu as pltpu
from jax.sharding import PartitionSpec as P

ITERS = 3
AXES = ("tiles", "rep")
distance_floor = 0.25
DIRECT_BYTES = 1 << 20
SHARED_BYTES = 2 << 20
BATCH = 4
CHIPS = 4
JOIN_BYTES = 1 << 28


def pieces(array, count):
    found = []
    for _ in range(count):
        piece = array.astype(jnp.bfloat16)
        found.append(piece)
        array = array - piece.astype(jnp.float32)
    return found


def products(points, ratios, axis):
    left = jnp.concatenate([piece.astype(jnp.float32) for piece in pieces(points, 3)]).astype(jnp.bfloat16)
    right = jnp.concatenate(ratios, axis=axis)
    split = lax.dot_general(
        jnp.concatenate([left] * len(ratios), axis=1),
        right,
        (((1,), (axis,)), ((), ())),
        preferred_element_type=jnp.float32,
    )
    return split[:8] + split[8:16] + split[16:]


def tile_terms(row_points, col_points, delta, kept, last):
    width = delta.shape[0]
    columns = row_points.T
    squared = jnp.zeros((width, width), jnp.float32)
    for k in range(3):
        spread = columns[:, k : k + 1] - col_points[k : k + 1, :]
        squared = squared + spread * spread
    squared = jnp.maximum(squared, distance_floor)
    inverse = lax.rsqrt(squared)
    ratios = jnp.where(kept, delta * inverse, jnp.float32(0.0))
    off = None
    if last:
        off = jnp.where(kept, delta - squared * inverse, jnp.float32(0.0))
        off = jnp.sum((off * off).reshape(-1, 8, width), axis=0)
    ratios = pieces(ratios, 2)
    to_rows = products(col_points, ratios, 1)
    to_cols = products(row_points, ratios, 0)
    return row_points * to_rows[3:4] - to_rows, col_points * to_cols[3:4] - to_cols, off


def placed(messages, block_count):
    blocks = []
    for b in range(block_count):
        found = jnp.zeros_like(messages[0])
        for message in messages:
            found = found + jnp.where(message[3:4] == b, message, jnp.float32(0.0))
        blocks.append(found)
    return blocks


def iteration(shared, first, last, scaling, map_ref, dissim_ref, *refs):
    *parts, out_ref, coords, totals, misfit, row_list, col_list, place_list = refs
    block_count, width = coords.shape[0], coords.shape[2]

    def note(count, chip, slot, place):
        row = map_ref[2 * chip, slot]
        row_list[count] = row
        col_list[count] = map_ref[2 * chip + 1, slot]
        place_list[count] = place
        return count + (row >= 0).astype(jnp.int32)

    slots = map_ref.shape[1]
    count = jnp.int32(0)
    if shared:
        me = lax.axis_index("tiles") * 2 + lax.axis_index("rep") // 2
        for n in range(CHIPS * slots):
            count = note(count, me ^ (n // slots), n % slots, n * width)
    else:
        count = lax.fori_loop(0, slots, lambda s, count: note(count, 0, s, s * width), count)
    for j in range(BATCH):
        row_list[count + j] = 0
        col_list[count + j] = 0
        place_list[count + j] = 0
    row_of = lax.broadcasted_iota(jnp.int32, (8, width), 0)
    if first:
        blocks = placed([parts[0][m] for m in range(0, parts[0].shape[0], 2)], block_count)
    else:
        components = [
            sum(part[p, k] for part in parts for p in range(part.shape[0])) / scaling for k in range(3)
        ]
    for b in range(block_count):
        if first:
            rows = blocks[b]
        else:
            rows = components[2][b : b + 1]
            for k in (1, 0):
                rows = jnp.where(row_of == k, components[k][b : b + 1], rows)
        coords[b] = jnp.where(row_of < 3, rows, jnp.where(row_of == 3, jnp.float32(1.0), jnp.float32(0.0)))
    totals[...] = jnp.zeros_like(totals)
    if last:
        misfit[...] = jnp.zeros_like(misfit)
    above_diag = lax.broadcasted_iota(jnp.int32, (width, width), 0) < lax.broadcasted_iota(
        jnp.int32, (width, width), 1
    )

    def batch(i, carry):
        found = []
        for j in range(BATCH):
            n = i * BATCH + j
            row, col = row_list[n], col_list[n]
            kept = (above_diag | (row != col)) & (n < count)
            delta = dissim_ref[pl.ds(pl.multiple_of(place_list[n], 8), width)]
            found.append((row, col, *tile_terms(coords[row], coords[col], delta, kept, last)))
        for row, col, to_row, to_col, off in found:
            totals[row] += to_row
            totals[col] += to_col
            if last:
                misfit[...] += off
        return carry

    lax.fori_loop(0, (count + BATCH - 1) // BATCH, batch, 0)
    for k in range(3):
        out_ref[0, k] = totals[:, k, :]
    if last:
        out_ref[0, 3, :8] = misfit[...]
        if block_count > 8:
            out_ref[0, 3, 8:] = jnp.zeros((block_count - 8, width), jnp.float32)


def contributions(shared, first, last, scaling, block_count, tile_map, dissim, parts):
    width = dissim.shape[1]
    return pl.pallas_call(
        functools.partial(iteration, shared, first, last, scaling),
        out_shape=jax.ShapeDtypeStruct((1, 4 if last else 3, block_count, width), jnp.float32),
        in_specs=[
            pl.BlockSpec(memory_space=pltpu.SMEM),
            *[pl.BlockSpec(memory_space=pltpu.VMEM)] * (1 + len(parts)),
        ],
        out_specs=pl.BlockSpec(memory_space=pltpu.VMEM),
        scratch_shapes=[
            pltpu.VMEM((block_count, 8, width), jnp.float32),
            pltpu.VMEM((block_count, 8, width), jnp.float32),
            pltpu.VMEM((8, width), jnp.float32),
            *[pltpu.SMEM((dissim.shape[0] // width + BATCH,), jnp.int32)] * 3,
        ],
        compiler_params=pltpu.CompilerParams(vmem_limit_bytes=32 << 20),
        name="iteration",
    )(tile_map, dissim, *parts)


def join(*refs):
    *shares, out_ref, sem = refs
    size = shares[0].shape[0]
    copies = [
        pltpu.make_async_copy(share, out_ref.at[pl.ds(n * size, size)], sem.at[n]) for n, share in enumerate(shares)
    ]
    for copy in copies:
        copy.start()
    for copy in copies:
        copy.wait()


def joined(shares):
    slots, *tile = shares[0].shape
    return pl.pallas_call(
        join,
        out_shape=jax.ShapeDtypeStruct((len(shares) * slots, *tile), jnp.float32),
        in_specs=[pl.BlockSpec(memory_space=pl.ANY)] * len(shares),
        out_specs=pl.BlockSpec(memory_space=pltpu.VMEM),
        scratch_shapes=[pltpu.SemaphoreType.DMA((len(shares),))],
        compiler_params=pltpu.CompilerParams(vmem_limit_bytes=8 << 20),
        cost_estimate=pl.CostEstimate(flops=0, bytes_accessed=JOIN_BYTES, transcendentals=0),
        name="join",
    )(*shares)


def announce(map_ref, owned_ref, start_ref, out_ref):
    shape = out_ref.shape[1:]
    lane = lax.broadcasted_iota(jnp.int32, shape, 1)
    row_of = lax.broadcasted_iota(jnp.int32, shape, 0)
    numbers = jnp.where(row_of == 3, owned_ref[0], 0)
    for k in range(2):
        for s in range(map_ref.shape[1]):
            numbers = jnp.where((lane == s) & (row_of == 4 + k), map_ref[k, s], numbers)
    message = numbers.astype(jnp.float32)
    for k in range(3):
        message = jnp.where(row_of == k, start_ref[k], message)
    for n in range(out_ref.shape[0]):
        out_ref[n] = message


def messages(chips, tile_map, owned_blocks, start_coords):
    return pl.pallas_call(
        announce,
        out_shape=jax.ShapeDtypeStruct((chips, 8, start_coords.shape[2]), jnp.float32),
        in_specs=[
            pl.BlockSpec(memory_space=pltpu.SMEM),
            pl.BlockSpec(memory_space=pltpu.SMEM),
            pl.BlockSpec(memory_space=pltpu.VMEM),
        ],
        out_specs=pl.BlockSpec(memory_space=pltpu.VMEM),
        compiler_params=pltpu.CompilerParams(vmem_limit_bytes=8 << 20),
        name="announce",
    )(tile_map, owned_blocks, start_coords.swapaxes(0, 1))


def finish(scaling, owned_ref, *refs):
    *parts, coords_ref, stress_ref = refs
    summed = [sum(part[p, k] for part in parts for p in range(part.shape[0])) for k in range(4)]
    row_of = lax.broadcasted_iota(jnp.int32, summed[0].shape, 0)
    for o in range(coords_ref.shape[1]):
        for k in range(3):
            mine = jnp.where(row_of == owned_ref[o], summed[k], jnp.float32(0.0))
            coords_ref[k, o : o + 1] = jnp.sum(mine, axis=0, keepdims=True) / scaling
    stress_ref[0, 0] = jnp.sum(summed[3])


def results(scaling, owned_blocks, parts):
    owned_count, width = owned_blocks.shape[0], parts[0].shape[-1]
    coords, stress = pl.pallas_call(
        functools.partial(finish, scaling),
        out_shape=[
            jax.ShapeDtypeStruct((3, owned_count, width), jnp.float32),
            jax.ShapeDtypeStruct((1, 1), jnp.float32),
        ],
        in_specs=[
            pl.BlockSpec(memory_space=pltpu.SMEM),
            *[pl.BlockSpec(memory_space=pltpu.VMEM)] * len(parts),
        ],
        out_specs=[pl.BlockSpec(memory_space=pltpu.VMEM), pl.BlockSpec(memory_space=pltpu.SMEM)],
        compiler_params=pltpu.CompilerParams(vmem_limit_bytes=8 << 20),
        name="finish",
    )(owned_blocks, *parts)
    return coords.swapaxes(0, 1), stress.reshape(())


def swapped(messages, chips):
    groups = [[2 * i + core for i in range(chips)] for core in range(2)]
    return lax.all_to_all(messages, AXES, 0, 0, axis_index_groups=groups)


def moved(array, devices, distance):
    return lax.ppermute(array, AXES, [(i, i ^ distance) for i in range(devices)])


def moved(array, devices, distance):
    return lax.ppermute(array, AXES, [(i, i ^ distance) for i in range(devices)])


def moved(array, devices, distance):
    return lax.ppermute(array, AXES, [(i, i ^ distance) for i in range(devices)])


def exchanged(message, tiles, rep, group):
    devices = tiles * rep
    if not group and (devices % 2 or devices // 2 * message.size * 4 > DIRECT_BYTES):
        return [lax.psum(message, AXES)]
    message = message + moved(message, devices, 1)
    if group:
        return [message] + [moved(message, devices, k) for k in range(group, devices, group)]
    return [swapped(jnp.broadcast_to(message, (devices // 2, *message.shape[1:])), devices // 2)]


def local(tiles, rep, dissim, tile_map, owned_blocks, start_coords):
    owned_count, _, width = start_coords.shape
    slots = dissim.shape[0]
    devices = tiles * rep
    block_count = owned_count * tiles
    scaling = float(block_count * width)
    tile_map = tile_map.T
    fits = CHIPS * dissim.size * 4 <= SHARED_BYTES
    if fits and rep == 4 and owned_count == 1 and tiles in (4, 8):
        group = 2 * CHIPS
        shares = [dissim] + [moved(dissim, devices, 2 * k) for k in range(1, CHIPS)]
        dissim = joined(shares)
        parts = [swapped(messages(devices // 2, tile_map, owned_blocks, start_coords), devices // 2)]
        parts[0], dissim = lax.optimization_barrier((parts[0], dissim))
        tile_map = parts[0][:, 4:6, :slots].astype(jnp.int32).reshape(-1, slots)
    else:
        group = 0
        named = lax.all_gather(owned_blocks, "tiles", tiled=True)
        parts = lax.all_gather(start_coords, "tiles", tiled=True)
        put = (named[None] == jnp.arange(block_count)[:, None]).astype(jnp.float32)
        parts = [jnp.einsum("bk,kcp->cbp", put, parts, precision=lax.Precision.HIGHEST)[None]]
    dissim = dissim.reshape(-1, width)
    for step in range(ITERS):
        first, last = step == 0, step == ITERS - 1
        totals = contributions(
            group > 0, group > 0 and first, last, 1.0 if first else scaling, block_count, tile_map, dissim, parts
        )
        parts = exchanged(totals, tiles, rep, group)
    return results(scaling, owned_blocks, parts)


def solution(mesh):
    return jax.shard_map(
        functools.partial(local, mesh.shape["tiles"], mesh.shape["rep"]),
        mesh=mesh,
        in_specs=(
            P(AXES, None, None),
            P(AXES, None),
            P("tiles"),
            P("tiles", None, None),
        ),
        out_specs=(P("tiles", None, None), P()),
        check_vma=False,
    )
```

```python
import functools

import jax
import jax.numpy as jnp
from jax import lax
from jax.experimental import pallas as pl
from jax.experimental.pallas import tpu as pltpu
from jax.sharding import PartitionSpec as P

ITERS = 3
AXES = ("tiles", "rep")
distance_floor = 0.25
DIRECT_BYTES = 1 << 20
SHARED_BYTES = 2 << 20
BATCH = 8
CHIPS = 4
JOIN_BYTES = 1 << 28


def pieces(array, count):
    found = []
    for _ in range(count):
        piece = array.astype(jnp.bfloat16)
        found.append(piece)
        array = array - piece.astype(jnp.float32)
    return found


def products(points, ratios, axis):
    left = jnp.concatenate([piece.astype(jnp.float32) for piece in pieces(points, 3)]).astype(jnp.bfloat16)
    right = jnp.concatenate(ratios, axis=axis)
    split = lax.dot_general(
        jnp.concatenate([left] * len(ratios), axis=1),
        right,
        (((1,), (axis,)), ((), ())),
        preferred_element_type=jnp.float32,
    )
    return split[:8] + split[8:16] + split[16:]


def tile_terms(row_points, col_points, delta, kept, last):
    width = delta.shape[0]
    columns = row_points.T
    squared = jnp.zeros((width, width), jnp.float32)
    for k in range(3):
        spread = columns[:, k : k + 1] - col_points[k : k + 1, :]
        squared = squared + spread * spread
    squared = jnp.maximum(squared, distance_floor)
    inverse = lax.rsqrt(squared)
    ratios = jnp.where(kept, delta * inverse, jnp.float32(0.0))
    off = None
    if last:
        off = jnp.where(kept, delta - squared * inverse, jnp.float32(0.0))
        off = jnp.sum((off * off).reshape(-1, 8, width), axis=0)
    ratios = pieces(ratios, 2)
    to_rows = products(col_points, ratios, 1)
    to_cols = products(row_points, ratios, 0)
    return row_points * to_rows[3:4] - to_rows, col_points * to_cols[3:4] - to_cols, off


def placed(messages, block_count):
    blocks = []
    for b in range(block_count):
        found = jnp.zeros_like(messages[0])
        for message in messages:
            found = found + jnp.where(message[3:4] == b, message, jnp.float32(0.0))
        blocks.append(found)
    return blocks


def iteration(shared, first, last, scaling, map_ref, dissim_ref, *refs):
    *parts, out_ref, coords, totals, misfit, row_list, col_list, place_list = refs
    block_count, width = coords.shape[0], coords.shape[2]

    def note(count, chip, slot, place):
        row = map_ref[2 * chip, slot]
        row_list[count] = row
        col_list[count] = map_ref[2 * chip + 1, slot]
        place_list[count] = place
        return count + (row >= 0).astype(jnp.int32)

    slots = map_ref.shape[1]
    count = jnp.int32(0)
    if shared:
        me, tiles = lax.axis_index("tiles"), map_ref.shape[0] // 2 - 2
        for n in range(CHIPS * slots):
            chip = (me, tiles, me ^ 1, tiles + 1)[n // slots]
            count = note(count, chip, n % slots, n * width)
    else:
        count = lax.fori_loop(0, slots, lambda s, count: note(count, 0, s, s * width), count)
    for j in range(BATCH):
        row_list[count + j] = 0
        col_list[count + j] = 0
        place_list[count + j] = 0
    row_of = lax.broadcasted_iota(jnp.int32, (8, width), 0)
    if first:
        blocks = placed([parts[0][m] for m in range(block_count)], block_count)
    else:
        components = [
            sum(part[p, k] for part in parts for p in range(part.shape[0])) / scaling for k in range(3)
        ]
    for b in range(block_count):
        if first:
            rows = blocks[b]
        else:
            rows = components[2][b : b + 1]
            for k in (1, 0):
                rows = jnp.where(row_of == k, components[k][b : b + 1], rows)
        coords[b] = jnp.where(row_of < 3, rows, jnp.where(row_of == 3, jnp.float32(1.0), jnp.float32(0.0)))
    totals[...] = jnp.zeros_like(totals)
    if last:
        misfit[...] = jnp.zeros_like(misfit)
    above_diag = lax.broadcasted_iota(jnp.int32, (width, width), 0) < lax.broadcasted_iota(
        jnp.int32, (width, width), 1
    )

    def batch(i, carry):
        found = []
        for j in range(BATCH):
            n = i * BATCH + j
            row, col = row_list[n], col_list[n]
            kept = (above_diag | (row != col)) & (n < count)
            delta = dissim_ref[pl.ds(pl.multiple_of(place_list[n], 8), width)]
            found.append((row, col, *tile_terms(coords[row], coords[col], delta, kept, last)))
        for row, col, to_row, to_col, off in found:
            totals[row] += to_row
            totals[col] += to_col
            if last:
                misfit[...] += off
        return carry

    lax.fori_loop(0, (count + BATCH - 1) // BATCH, batch, 0)
    for k in range(3):
        out_ref[0, k] = totals[:, k, :]
    if last:
        out_ref[0, 3, :8] = misfit[...]
        if block_count > 8:
            out_ref[0, 3, 8:] = jnp.zeros((block_count - 8, width), jnp.float32)


def contributions(shared, first, last, scaling, block_count, tile_map, dissim, parts):
    width = dissim.shape[1]
    return pl.pallas_call(
        functools.partial(iteration, shared, first, last, scaling),
        out_shape=jax.ShapeDtypeStruct((1, 4 if last else 3, block_count, width), jnp.float32),
        in_specs=[
            pl.BlockSpec(memory_space=pltpu.SMEM),
            *[pl.BlockSpec(memory_space=pltpu.VMEM)] * (1 + len(parts)),
        ],
        out_specs=pl.BlockSpec(memory_space=pltpu.VMEM),
        scratch_shapes=[
            pltpu.VMEM((block_count, 8, width), jnp.float32),
            pltpu.VMEM((block_count, 8, width), jnp.float32),
            pltpu.VMEM((8, width), jnp.float32),
            *[pltpu.SMEM((dissim.shape[0] // width + BATCH,), jnp.int32)] * 3,
        ],
        compiler_params=pltpu.CompilerParams(vmem_limit_bytes=32 << 20),
        name="iteration",
    )(tile_map, dissim, *parts)


def join(*refs):
    *shares, out_ref, sem = refs
    size = shares[0].shape[0]
    copies = [
        pltpu.make_async_copy(share, out_ref.at[pl.ds(n * size, size)], sem.at[n]) for n, share in enumerate(shares)
    ]
    for copy in copies:
        copy.start()
    for copy in copies:
        copy.wait()


def joined(shares):
    slots, *tile = shares[0].shape
    return pl.pallas_call(
        join,
        out_shape=jax.ShapeDtypeStruct((len(shares) * slots, *tile), jnp.float32),
        in_specs=[pl.BlockSpec(memory_space=pl.ANY)] * len(shares),
        out_specs=pl.BlockSpec(memory_space=pltpu.VMEM),
        scratch_shapes=[pltpu.SemaphoreType.DMA((len(shares),))],
        compiler_params=pltpu.CompilerParams(vmem_limit_bytes=8 << 20),
        cost_estimate=pl.CostEstimate(flops=0, bytes_accessed=JOIN_BYTES, transcendentals=0),
        name="join",
    )(*shares)


def announce(map_ref, owned_ref, start_ref, out_ref, copies_ref):
    lane = lax.broadcasted_iota(jnp.int32, out_ref.shape, 1)
    row_of = lax.broadcasted_iota(jnp.int32, out_ref.shape, 0)
    numbers = jnp.where(row_of == 3, owned_ref[0], 0)
    for k in range(2):
        for s in range(map_ref.shape[1]):
            numbers = jnp.where((lane == s) & (row_of == 4 + k), map_ref[k, s], numbers)
    message = numbers.astype(jnp.float32)
    for k in range(3):
        message = jnp.where(row_of == k, start_ref[k], message)
    out_ref[...] = message
    for n in range(copies_ref.shape[0]):
        copies_ref[n] = message


def messages(tiles, tile_map, owned_blocks, start_coords):
    shape = (8, start_coords.shape[2])
    return pl.pallas_call(
        announce,
        out_shape=[jax.ShapeDtypeStruct(shape, jnp.float32), jax.ShapeDtypeStruct((tiles, *shape), jnp.float32)],
        in_specs=[
            pl.BlockSpec(memory_space=pltpu.SMEM),
            pl.BlockSpec(memory_space=pltpu.SMEM),
            pl.BlockSpec(memory_space=pltpu.VMEM),
        ],
        out_specs=[pl.BlockSpec(memory_space=pltpu.VMEM)] * 2,
        compiler_params=pltpu.CompilerParams(vmem_limit_bytes=8 << 20),
        name="announce",
    )(tile_map, owned_blocks, start_coords.swapaxes(0, 1))


def finish(scaling, owned_ref, *refs):
    *parts, coords_ref, stress_ref = refs
    summed = [sum(part[p, k] for part in parts for p in range(part.shape[0])) for k in range(4)]
    row_of = lax.broadcasted_iota(jnp.int32, summed[0].shape, 0)
    for o in range(coords_ref.shape[1]):
        for k in range(3):
            mine = jnp.where(row_of == owned_ref[o], summed[k], jnp.float32(0.0))
            coords_ref[k, o : o + 1] = jnp.sum(mine, axis=0, keepdims=True) / scaling
    stress_ref[0, 0] = jnp.sum(summed[3])


def results(scaling, owned_blocks, parts):
    owned_count, width = owned_blocks.shape[0], parts[0].shape[-1]
    coords, stress = pl.pallas_call(
        functools.partial(finish, scaling),
        out_shape=[
            jax.ShapeDtypeStruct((3, owned_count, width), jnp.float32),
            jax.ShapeDtypeStruct((1, 1), jnp.float32),
        ],
        in_specs=[
            pl.BlockSpec(memory_space=pltpu.SMEM),
            *[pl.BlockSpec(memory_space=pltpu.VMEM)] * len(parts),
        ],
        out_specs=[pl.BlockSpec(memory_space=pltpu.VMEM), pl.BlockSpec(memory_space=pltpu.SMEM)],
        compiler_params=pltpu.CompilerParams(vmem_limit_bytes=8 << 20),
        name="finish",
    )(owned_blocks, *parts)
    return coords.swapaxes(0, 1), stress.reshape(())


def swapped(messages, chips):
    groups = [[2 * i + core for i in range(chips)] for core in range(2)]
    return lax.all_to_all(messages, AXES, 0, 0, axis_index_groups=groups)


def moved(array, devices, distance):
    return lax.ppermute(array, AXES, [(i, i ^ distance) for i in range(devices)])


def moved(array, devices, distance):
    return lax.ppermute(array, AXES, [(i, i ^ distance) for i in range(devices)])


def moved(array, devices, distance):
    return lax.ppermute(array, AXES, [(i, i ^ distance) for i in range(devices)])


def exchanged(message, tiles, rep, group):
    devices = tiles * rep
    if not group and (devices % 2 or devices // 2 * message.size * 4 > DIRECT_BYTES):
        return [lax.psum(message, AXES)]
    message = message + moved(message, devices, 1)
    if group:
        return [message] + [moved(message, devices, k) for k in range(group, devices, group)]
    return [swapped(jnp.broadcast_to(message, (devices // 2, *message.shape[1:])), devices // 2)]


def local(tiles, rep, dissim, tile_map, owned_blocks, start_coords):
    owned_count, _, width = start_coords.shape
    slots = dissim.shape[0]
    devices = tiles * rep
    block_count = owned_count * tiles
    scaling = float(block_count * width)
    tile_map = tile_map.T
    fits = CHIPS * dissim.size * 4 <= SHARED_BYTES
    if fits and rep == 4 and owned_count == 1 and tiles in (4, 8):
        group = 2 * CHIPS
        far, other = rep // 2, rep
        message, copies = messages(tiles, tile_map, owned_blocks, start_coords)
        parts = [lax.all_to_all(copies, "tiles", 0, 0)]
        maps = [moved(message, devices, k) for k in (far, far + other)]
        dissim = joined([dissim] + [moved(dissim, devices, k) for k in (far, other, far + other)])
        parts, maps, dissim = lax.optimization_barrier((parts, maps, dissim))
        tile_map = jnp.concatenate([parts[0], jnp.stack(maps)])[:, 4:6, :slots].astype(jnp.int32).reshape(-1, slots)
    else:
        group = 0
        named = lax.all_gather(owned_blocks, "tiles", tiled=True)
        parts = lax.all_gather(start_coords, "tiles", tiled=True)
        put = (named[None] == jnp.arange(block_count)[:, None]).astype(jnp.float32)
        parts = [jnp.einsum("bk,kcp->cbp", put, parts, precision=lax.Precision.HIGHEST)[None]]
    dissim = dissim.reshape(-1, width)
    for step in range(ITERS):
        first, last = step == 0, step == ITERS - 1
        totals = contributions(
            group > 0, group > 0 and first, last, 1.0 if first else scaling, block_count, tile_map, dissim, parts
        )
        parts = exchanged(totals, tiles, rep, group)
    return results(scaling, owned_blocks, parts)


def solution(mesh):
    return jax.shard_map(
        functools.partial(local, mesh.shape["tiles"], mesh.shape["rep"]),
        mesh=mesh,
        in_specs=(
            P(AXES, None, None),
            P(AXES, None),
            P("tiles"),
            P("tiles", None, None),
        ),
        out_specs=(P("tiles", None, None), P()),
        check_vma=False,
    )
```

```python
import functools

import jax
import jax.numpy as jnp
from jax import lax
from jax.experimental import pallas as pl
from jax.experimental.pallas import tpu as pltpu
from jax.sharding import PartitionSpec as P

ITERS = 3
AXES = ("tiles", "rep")
distance_floor = 0.25
DIRECT_BYTES = 1 << 20
SHARED_BYTES = 2 << 20
BATCH = 8
CHIPS = 4
JOIN_BYTES = 1 << 28


def pieces(array, count):
    found = []
    for _ in range(count):
        piece = array.astype(jnp.bfloat16)
        found.append(piece)
        array = array - piece.astype(jnp.float32)
    return found


def products(points, ratios, axis):
    left = jnp.concatenate([piece.astype(jnp.float32) for piece in pieces(points, 3)]).astype(jnp.bfloat16)
    right = jnp.concatenate(ratios, axis=axis)
    split = lax.dot_general(
        jnp.concatenate([left] * len(ratios), axis=1),
        right,
        (((1,), (axis,)), ((), ())),
        preferred_element_type=jnp.float32,
    )
    return split[:8] + split[8:16] + split[16:]


def tile_terms(row_points, col_points, delta, kept, last):
    width = delta.shape[0]
    columns = row_points.T
    squared = jnp.zeros((width, width), jnp.float32)
    for k in range(3):
        spread = columns[:, k : k + 1] - col_points[k : k + 1, :]
        squared = squared + spread * spread
    squared = jnp.maximum(squared, distance_floor)
    inverse = lax.rsqrt(squared)
    ratios = jnp.where(kept, delta * inverse, jnp.float32(0.0))
    off = None
    if last:
        off = jnp.where(kept, delta - squared * inverse, jnp.float32(0.0))
        off = jnp.sum((off * off).reshape(-1, 8, width), axis=0)
    ratios = pieces(ratios, 2)
    to_rows = products(col_points, ratios, 1)
    to_cols = products(row_points, ratios, 0)
    return row_points * to_rows[3:4] - to_rows, col_points * to_cols[3:4] - to_cols, off


def placed(messages, block_count):
    blocks = []
    for b in range(block_count):
        found = jnp.zeros_like(messages[0])
        for message in messages:
            found = found + jnp.where(message[3:4] == b, message, jnp.float32(0.0))
        blocks.append(found)
    return blocks


def iteration(shared, first, last, scaling, map_ref, dissim_ref, *refs):
    *parts, out_ref, coords, totals, misfit, row_list, col_list, place_list = refs
    block_count, width = coords.shape[0], coords.shape[2]

    def note(count, chip, slot, place):
        row = map_ref[2 * chip, slot]
        row_list[count] = row
        col_list[count] = map_ref[2 * chip + 1, slot]
        place_list[count] = place
        return count + (row >= 0).astype(jnp.int32)

    slots = map_ref.shape[1]
    count = jnp.int32(0)
    if shared:
        me, tiles = lax.axis_index("tiles"), map_ref.shape[0] // 2 - 2
        for n in range(CHIPS * slots):
            chip = (me, tiles, me ^ 1, tiles + 1)[n // slots]
            count = note(count, chip, n % slots, n * width)
    else:
        count = lax.fori_loop(0, slots, lambda s, count: note(count, 0, s, s * width), count)
    for j in range(BATCH):
        row_list[count + j] = 0
        col_list[count + j] = 0
        place_list[count + j] = 0
    row_of = lax.broadcasted_iota(jnp.int32, (8, width), 0)
    if first:
        blocks = placed([parts[0][m] for m in range(block_count)], block_count)
    else:
        components = [
            sum(part[p, k] for part in parts for p in range(part.shape[0])) / scaling for k in range(3)
        ]
    for b in range(block_count):
        if first:
            rows = blocks[b]
        else:
            rows = components[2][b : b + 1]
            for k in (1, 0):
                rows = jnp.where(row_of == k, components[k][b : b + 1], rows)
        coords[b] = jnp.where(row_of < 3, rows, jnp.where(row_of == 3, jnp.float32(1.0), jnp.float32(0.0)))
    totals[...] = jnp.zeros_like(totals)
    if last:
        misfit[...] = jnp.zeros_like(misfit)
    above_diag = lax.broadcasted_iota(jnp.int32, (width, width), 0) < lax.broadcasted_iota(
        jnp.int32, (width, width), 1
    )

    def batch(i, carry):
        found = []
        for j in range(BATCH):
            n = i * BATCH + j
            row, col = row_list[n], col_list[n]
            kept = (above_diag | (row != col)) & (n < count)
            delta = dissim_ref[pl.ds(pl.multiple_of(place_list[n], 8), width)]
            found.append((row, col, *tile_terms(coords[row], coords[col], delta, kept, last)))
        for row, col, to_row, to_col, off in found:
            totals[row] += to_row
            totals[col] += to_col
            if last:
                misfit[...] += off
        return carry

    lax.fori_loop(0, (count + BATCH - 1) // BATCH, batch, 0)
    for k in range(3):
        out_ref[0, k] = totals[:, k, :]
    if last:
        out_ref[0, 3, :8] = misfit[...]
        if block_count > 8:
            out_ref[0, 3, 8:] = jnp.zeros((block_count - 8, width), jnp.float32)


def contributions(shared, first, last, scaling, block_count, tile_map, dissim, parts):
    width = dissim.shape[1]
    return pl.pallas_call(
        functools.partial(iteration, shared, first, last, scaling),
        out_shape=jax.ShapeDtypeStruct((1, 4 if last else 3, block_count, width), jnp.float32),
        in_specs=[
            pl.BlockSpec(memory_space=pltpu.SMEM),
            *[pl.BlockSpec(memory_space=pltpu.VMEM)] * (1 + len(parts)),
        ],
        out_specs=pl.BlockSpec(memory_space=pltpu.VMEM),
        scratch_shapes=[
            pltpu.VMEM((block_count, 8, width), jnp.float32),
            pltpu.VMEM((block_count, 8, width), jnp.float32),
            pltpu.VMEM((8, width), jnp.float32),
            *[pltpu.SMEM((dissim.shape[0] // width + BATCH,), jnp.int32)] * 3,
        ],
        compiler_params=pltpu.CompilerParams(vmem_limit_bytes=32 << 20),
        name="iteration",
    )(tile_map, dissim, *parts)


def join(*refs):
    _, *shares, out_ref, sem = refs
    size = shares[0].shape[0]
    copies = [
        pltpu.make_async_copy(share, out_ref.at[pl.ds((n + 1) * size, size)], sem.at[n])
        for n, share in enumerate(shares)
    ]
    for copy in copies:
        copy.start()
    for copy in copies:
        copy.wait()


def joined(room, shares):
    return pl.pallas_call(
        join,
        out_shape=jax.ShapeDtypeStruct(room.shape, room.dtype),
        in_specs=[pl.BlockSpec(memory_space=pl.ANY)] * (1 + len(shares)),
        out_specs=pl.BlockSpec(memory_space=pl.ANY),
        scratch_shapes=[pltpu.SemaphoreType.DMA((len(shares),))],
        input_output_aliases={0: 0},
        compiler_params=pltpu.CompilerParams(vmem_limit_bytes=8 << 20),
        cost_estimate=pl.CostEstimate(flops=0, bytes_accessed=JOIN_BYTES, transcendentals=0),
        name="join",
    )(room, *shares)


def finish(scaling, owned_ref, *refs):
    *parts, coords_ref, stress_ref = refs
    summed = [sum(part[p, k] for part in parts for p in range(part.shape[0])) for k in range(4)]
    row_of = lax.broadcasted_iota(jnp.int32, summed[0].shape, 0)
    for o in range(coords_ref.shape[1]):
        for k in range(3):
            mine = jnp.where(row_of == owned_ref[o], summed[k], jnp.float32(0.0))
            coords_ref[k, o : o + 1] = jnp.sum(mine, axis=0, keepdims=True) / scaling
    stress_ref[0, 0] = jnp.sum(summed[3])


def results(scaling, owned_blocks, parts):
    owned_count, width = owned_blocks.shape[0], parts[0].shape[-1]
    coords, stress = pl.pallas_call(
        functools.partial(finish, scaling),
        out_shape=[
            jax.ShapeDtypeStruct((3, owned_count, width), jnp.float32),
            jax.ShapeDtypeStruct((1, 1), jnp.float32),
        ],
        in_specs=[
            pl.BlockSpec(memory_space=pltpu.SMEM),
            *[pl.BlockSpec(memory_space=pltpu.VMEM)] * len(parts),
        ],
        out_specs=[pl.BlockSpec(memory_space=pltpu.VMEM), pl.BlockSpec(memory_space=pltpu.SMEM)],
        compiler_params=pltpu.CompilerParams(vmem_limit_bytes=8 << 20),
        name="finish",
    )(owned_blocks, *parts)
    return coords.swapaxes(0, 1), stress.reshape(())


def swapped(messages, chips):
    groups = [[2 * i + core for i in range(chips)] for core in range(2)]
    return lax.all_to_all(messages, AXES, 0, 0, axis_index_groups=groups)


def moved(array, devices, distance):
    return lax.ppermute(array, AXES, [(i, i ^ distance) for i in range(devices)])


def moved(array, devices, distance):
    return lax.ppermute(array, AXES, [(i, i ^ distance) for i in range(devices)])


def moved(array, devices, distance):
    return lax.ppermute(array, AXES, [(i, i ^ distance) for i in range(devices)])


def exchanged(message, tiles, rep, group):
    devices = tiles * rep
    if not group and (devices % 2 or devices // 2 * message.size * 4 > DIRECT_BYTES):
        return [lax.psum(message, AXES)]
    message = message + moved(message, devices, 1)
    if group:
        return [message] + [moved(message, devices, k) for k in range(group, devices, group)]
    return [swapped(jnp.broadcast_to(message, (devices // 2, *message.shape[1:])), devices // 2)]


def local(tiles, rep, dissim, tile_map, owned_blocks, start_coords):
    owned_count, _, width = start_coords.shape
    slots = dissim.shape[0]
    devices = tiles * rep
    block_count = owned_count * tiles
    scaling = float(block_count * width)
    tile_map = tile_map.T
    fits = CHIPS * dissim.size * 4 <= SHARED_BYTES
    if fits and rep == 4 and owned_count == 1 and tiles in (4, 8):
        group = 2 * CHIPS
        far, other = rep // 2, rep
        numbers = jnp.pad(tile_map.astype(jnp.float32), ((0, 2), (0, width - slots)))
        block = jnp.full((1, width), owned_blocks[0], jnp.float32)
        message = jnp.concatenate([start_coords[0], block, numbers])
        copies = jnp.broadcast_to(message, (tiles, 8, width))
        parts = [lax.all_to_all(copies, "tiles", 0, 0)]
        room = jnp.pad(dissim, ((0, (CHIPS - 1) * slots), (0, 0), (0, 0)))
        maps = [moved(message, devices, k) for k in (far, far + other)]
        dissim = joined(room, [moved(dissim, devices, k) for k in (far, other, far + other)])
        parts, maps, dissim = lax.optimization_barrier((parts, maps, dissim))
        tile_map = jnp.concatenate([parts[0], jnp.stack(maps)])[:, 4:6, :slots].astype(jnp.int32).reshape(-1, slots)
    else:
        group = 0
        named = lax.all_gather(owned_blocks, "tiles", tiled=True)
        parts = lax.all_gather(start_coords, "tiles", tiled=True)
        put = (named[None] == jnp.arange(block_count)[:, None]).astype(jnp.float32)
        parts = [jnp.einsum("bk,kcp->cbp", put, parts, precision=lax.Precision.HIGHEST)[None]]
    dissim = dissim.reshape(-1, width)
    for step in range(ITERS):
        first, last = step == 0, step == ITERS - 1
        totals = contributions(
            group > 0, group > 0 and first, last, 1.0 if first else scaling, block_count, tile_map, dissim, parts
        )
        parts = exchanged(totals, tiles, rep, group)
    return results(scaling, owned_blocks, parts)


def solution(mesh):
    return jax.shard_map(
        functools.partial(local, mesh.shape["tiles"], mesh.shape["rep"]),
        mesh=mesh,
        in_specs=(
            P(AXES, None, None),
            P(AXES, None),
            P("tiles"),
            P("tiles", None, None),
        ),
        out_specs=(P("tiles", None, None), P()),
        check_vma=False,
    )
```

```python
import functools

import jax
import jax.numpy as jnp
from jax import lax
from jax.experimental import pallas as pl
from jax.experimental.pallas import tpu as pltpu
from jax.sharding import PartitionSpec as P

ITERS = 3
AXES = ("tiles", "rep")
distance_floor = 0.25
DIRECT_BYTES = 1 << 20
SHARED_BYTES = 2 << 20
BATCH = 6
CHIPS = 4
JOIN_BYTES = 1 << 28


def pieces(array, count):
    found = []
    for _ in range(count):
        piece = array.astype(jnp.bfloat16)
        found.append(piece)
        array = array - piece.astype(jnp.float32)
    return found


def products(points, ratios, axis):
    left = jnp.concatenate([piece.astype(jnp.float32) for piece in pieces(points, 3)]).astype(jnp.bfloat16)
    right = jnp.concatenate(ratios, axis=axis)
    split = lax.dot_general(
        jnp.concatenate([left] * len(ratios), axis=1),
        right,
        (((1,), (axis,)), ((), ())),
        preferred_element_type=jnp.float32,
    )
    return split[:8] + split[8:16] + split[16:]


def tile_terms(row_points, col_points, delta, kept, last):
    width = delta.shape[0]
    columns = row_points.T
    squared = jnp.zeros((width, width), jnp.float32)
    for k in range(3):
        spread = columns[:, k : k + 1] - col_points[k : k + 1, :]
        squared = squared + spread * spread
    squared = jnp.maximum(squared, distance_floor)
    inverse = lax.rsqrt(squared)
    ratios = jnp.where(kept, delta * inverse, jnp.float32(0.0))
    off = None
    if last:
        off = jnp.where(kept, delta - squared * inverse, jnp.float32(0.0))
        off = jnp.sum((off * off).reshape(-1, 8, width), axis=0)
    ratios = pieces(ratios, 2)
    to_rows = products(col_points, ratios, 1)
    to_cols = products(row_points, ratios, 0)
    return row_points * to_rows[3:4] - to_rows, col_points * to_cols[3:4] - to_cols, off


def placed(messages, block_count):
    blocks = []
    for b in range(block_count):
        found = jnp.zeros_like(messages[0])
        for message in messages:
            found = found + jnp.where(message[3:4] == b, message, jnp.float32(0.0))
        blocks.append(found)
    return blocks


def iteration(shared, first, last, scaling, map_ref, dissim_ref, *refs):
    *parts, out_ref, coords, totals, misfit, row_list, col_list, place_list = refs
    block_count, width = coords.shape[0], coords.shape[2]

    def note(count, chip, slot, place):
        row = map_ref[2 * chip, slot]
        row_list[count] = row
        col_list[count] = map_ref[2 * chip + 1, slot]
        place_list[count] = place
        return count + (row >= 0).astype(jnp.int32)

    slots = map_ref.shape[1]
    count = jnp.int32(0)
    if shared:
        me, tiles = lax.axis_index("tiles"), map_ref.shape[0] // 2 - 2
        for n in range(CHIPS * slots):
            chip = (me, tiles, me ^ 1, tiles + 1)[n // slots]
            count = note(count, chip, n % slots, n * width)
    else:
        count = lax.fori_loop(0, slots, lambda s, count: note(count, 0, s, s * width), count)
    for j in range(BATCH):
        row_list[count + j] = 0
        col_list[count + j] = 0
        place_list[count + j] = 0
    row_of = lax.broadcasted_iota(jnp.int32, (8, width), 0)
    if first:
        blocks = placed([parts[0][m] for m in range(block_count)], block_count)
    else:
        components = [
            sum(part[p, k] for part in parts for p in range(part.shape[0])) / scaling for k in range(3)
        ]
    for b in range(block_count):
        if first:
            rows = blocks[b]
        else:
            rows = components[2][b : b + 1]
            for k in (1, 0):
                rows = jnp.where(row_of == k, components[k][b : b + 1], rows)
        coords[b] = jnp.where(row_of < 3, rows, jnp.where(row_of == 3, jnp.float32(1.0), jnp.float32(0.0)))
    totals[...] = jnp.zeros_like(totals)
    if last:
        misfit[...] = jnp.zeros_like(misfit)
    above_diag = lax.broadcasted_iota(jnp.int32, (width, width), 0) < lax.broadcasted_iota(
        jnp.int32, (width, width), 1
    )

    def batch(i, carry):
        found = []
        for j in range(BATCH):
            n = i * BATCH + j
            row, col = row_list[n], col_list[n]
            kept = (above_diag | (row != col)) & (n < count)
            delta = dissim_ref[pl.ds(pl.multiple_of(place_list[n], 8), width)]
            found.append((row, col, *tile_terms(coords[row], coords[col], delta, kept, last)))
        for row, col, to_row, to_col, off in found:
            totals[row] += to_row
            totals[col] += to_col
            if last:
                misfit[...] += off
        return carry

    lax.fori_loop(0, (count + BATCH - 1) // BATCH, batch, 0)
    for k in range(3):
        out_ref[0, k] = totals[:, k, :]
    if last:
        out_ref[0, 3, :8] = misfit[...]
        if block_count > 8:
            out_ref[0, 3, 8:] = jnp.zeros((block_count - 8, width), jnp.float32)


def contributions(shared, first, last, scaling, block_count, tile_map, dissim, parts):
    width = dissim.shape[1]
    return pl.pallas_call(
        functools.partial(iteration, shared, first, last, scaling),
        out_shape=jax.ShapeDtypeStruct((1, 4 if last else 3, block_count, width), jnp.float32),
        in_specs=[
            pl.BlockSpec(memory_space=pltpu.SMEM),
            *[pl.BlockSpec(memory_space=pltpu.VMEM)] * (1 + len(parts)),
        ],
        out_specs=pl.BlockSpec(memory_space=pltpu.VMEM),
        scratch_shapes=[
            pltpu.VMEM((block_count, 8, width), jnp.float32),
            pltpu.VMEM((block_count, 8, width), jnp.float32),
            pltpu.VMEM((8, width), jnp.float32),
            *[pltpu.SMEM((dissim.shape[0] // width + BATCH,), jnp.int32)] * 3,
        ],
        compiler_params=pltpu.CompilerParams(vmem_limit_bytes=32 << 20),
        name="iteration",
    )(tile_map, dissim, *parts)


def join(*refs):
    _, *shares, out_ref, sem = refs
    size = shares[0].shape[0]
    copies = [
        pltpu.make_async_copy(share, out_ref.at[pl.ds((n + 1) * size, size)], sem.at[n])
        for n, share in enumerate(shares)
    ]
    for copy in copies:
        copy.start()
    for copy in copies:
        copy.wait()


def joined(room, shares):
    return pl.pallas_call(
        join,
        out_shape=jax.ShapeDtypeStruct(room.shape, room.dtype),
        in_specs=[pl.BlockSpec(memory_space=pl.ANY)] * (1 + len(shares)),
        out_specs=pl.BlockSpec(memory_space=pl.ANY),
        scratch_shapes=[pltpu.SemaphoreType.DMA((len(shares),))],
        input_output_aliases={0: 0},
        compiler_params=pltpu.CompilerParams(vmem_limit_bytes=8 << 20),
        cost_estimate=pl.CostEstimate(flops=0, bytes_accessed=JOIN_BYTES, transcendentals=0),
        name="join",
    )(room, *shares)


def finish(scaling, owned_ref, *refs):
    *parts, coords_ref, stress_ref = refs
    summed = [sum(part[p, k] for part in parts for p in range(part.shape[0])) for k in range(4)]
    row_of = lax.broadcasted_iota(jnp.int32, summed[0].shape, 0)
    for o in range(coords_ref.shape[1]):
        for k in range(3):
            mine = jnp.where(row_of == owned_ref[o], summed[k], jnp.float32(0.0))
            coords_ref[k, o : o + 1] = jnp.sum(mine, axis=0, keepdims=True) / scaling
    stress_ref[0, 0] = jnp.sum(summed[3])


def results(scaling, owned_blocks, parts):
    owned_count, width = owned_blocks.shape[0], parts[0].shape[-1]
    coords, stress = pl.pallas_call(
        functools.partial(finish, scaling),
        out_shape=[
            jax.ShapeDtypeStruct((3, owned_count, width), jnp.float32),
            jax.ShapeDtypeStruct((1, 1), jnp.float32),
        ],
        in_specs=[
            pl.BlockSpec(memory_space=pltpu.SMEM),
            *[pl.BlockSpec(memory_space=pltpu.VMEM)] * len(parts),
        ],
        out_specs=[pl.BlockSpec(memory_space=pltpu.VMEM), pl.BlockSpec(memory_space=pltpu.SMEM)],
        compiler_params=pltpu.CompilerParams(vmem_limit_bytes=8 << 20),
        name="finish",
    )(owned_blocks, *parts)
    return coords.swapaxes(0, 1), stress.reshape(())


def swapped(messages, chips):
    groups = [[2 * i + core for i in range(chips)] for core in range(2)]
    return lax.all_to_all(messages, AXES, 0, 0, axis_index_groups=groups)


def moved(array, devices, distance):
    return lax.ppermute(array, AXES, [(i, i ^ distance) for i in range(devices)])


def moved(array, devices, distance):
    return lax.ppermute(array, AXES, [(i, i ^ distance) for i in range(devices)])


def moved(array, devices, distance):
    return lax.ppermute(array, AXES, [(i, i ^ distance) for i in range(devices)])


def exchanged(message, tiles, rep, group):
    devices = tiles * rep
    if not group and (devices % 2 or devices // 2 * message.size * 4 > DIRECT_BYTES):
        return [lax.psum(message, AXES)]
    message = message + moved(message, devices, 1)
    if group:
        return [message] + [moved(message, devices, k) for k in range(group, devices, group)]
    return [swapped(jnp.broadcast_to(message, (devices // 2, *message.shape[1:])), devices // 2)]


def local(tiles, rep, dissim, tile_map, owned_blocks, start_coords):
    owned_count, _, width = start_coords.shape
    slots = dissim.shape[0]
    devices = tiles * rep
    block_count = owned_count * tiles
    scaling = float(block_count * width)
    tile_map = tile_map.T
    fits = CHIPS * dissim.size * 4 <= SHARED_BYTES
    if fits and rep == 4 and owned_count == 1 and tiles in (4, 8):
        group = 2 * CHIPS
        far, other = rep // 2, rep
        numbers = jnp.pad(tile_map.astype(jnp.float32), ((0, 2), (0, width - slots)))
        block = jnp.full((1, width), owned_blocks[0], jnp.float32)
        message = jnp.concatenate([start_coords[0], block, numbers])
        copies = jnp.broadcast_to(message, (tiles, 8, width))
        parts = [lax.all_to_all(copies, "tiles", 0, 0)]
        room = jnp.pad(dissim, ((0, (CHIPS - 1) * slots), (0, 0), (0, 0)))
        maps = [moved(message, devices, k) for k in (far, far + other)]
        dissim = joined(room, [moved(dissim, devices, k) for k in (far, other, far + other)])
        parts, maps, dissim = lax.optimization_barrier((parts, maps, dissim))
        tile_map = jnp.concatenate([parts[0], jnp.stack(maps)])[:, 4:6, :slots].astype(jnp.int32).reshape(-1, slots)
    else:
        group = 0
        named = lax.all_gather(owned_blocks, "tiles", tiled=True)
        parts = lax.all_gather(start_coords, "tiles", tiled=True)
        put = (named[None] == jnp.arange(block_count)[:, None]).astype(jnp.float32)
        parts = [jnp.einsum("bk,kcp->cbp", put, parts, precision=lax.Precision.HIGHEST)[None]]
    dissim = dissim.reshape(-1, width)
    for step in range(ITERS):
        first, last = step == 0, step == ITERS - 1
        totals = contributions(
            group > 0, group > 0 and first, last, 1.0 if first else scaling, block_count, tile_map, dissim, parts
        )
        parts = exchanged(totals, tiles, rep, group)
    return results(scaling, owned_blocks, parts)


def solution(mesh):
    return jax.shard_map(
        functools.partial(local, mesh.shape["tiles"], mesh.shape["rep"]),
        mesh=mesh,
        in_specs=(
            P(AXES, None, None),
            P(AXES, None),
            P("tiles"),
            P("tiles", None, None),
        ),
        out_specs=(P("tiles", None, None), P()),
        check_vma=False,
    )
```
